256 devices in a mesh: dom: 64 (over x, y_hi, z), pot: 4 (over y_lo, core).
Axes of the slice: x: 4, y: 4 (y_hi: 2, y_lo: 2; y = y_hi * 2 + y_lo), z: 8, core: 2. Of those that a mesh axis runs over, the one named last changes fastest.
Arguments:
- band_orbitals: float32 [4, 128, 192, 128], P(None, 'dom'), may hold values from -7 to 11, as said below
- local_potential: float32 [128, 192, 128], P('dom'), may hold values from 0.2 to 2
- band_shift: float32 [4], replicated, may hold values from 0.1 to 1
- trial_potentials: float32 [8, 128, 192, 128], P('pot', 'dom'), may hold values from -0.5 to 2
- projector_blocks: float32 [8, 2, 192, 128], replicated, may hold values from 0.2 to 1.8
- atom_plane: int32 [8], replicated, may hold values from 0 to 126, as said below
- projector_weight: float32 [8], replicated, may hold values from 0.5 to 4
Outputs:
- solution: float32 [8, 4, 128, 192, 128], P('pot', None, 'dom')
- response: float32 [8, 8], P('pot')
The draws below stay inside these ranges and needn't reach their ends.
Inputs may be any that keep to these rules, and one draw needn't show every extreme that they name: `band_orbitals`: orbitals of the nanocrystal's occupied bands. The block of atom a covers planes atom_plane[a] to atom_plane[a] + 1.
All inputs are finite; a program needn't handle non-finite values.
Results may differ from the reference program's by a relative error of at most 0.0003.
Values sent between devices are 32-bit elements; how exact they have to be, the bound alone decides.
A program may use at most 128 MiB of HBM per device.

```python
import math
import jax
import jax.numpy as jnp
from jax import lax

NY = 192
NZ = 128
NB = 4
KATOMS = 8
SPAN = 2
ITERS = 2
NX = 128
POTS = 8


def draw_band_orbitals(key, part):
    key = jax.random.fold_in(key, 11)
    places = jnp.arange(NX, dtype=jnp.float32) / max(NX - 1, 1)
    envelope = jnp.exp(math.log(3.0) * places)
    values = 0.7 + 0.7 * jnp.clip(jax.random.normal(key, (NB, NX, NY, NZ), jnp.float32), -4.0, 4.0)
    return (values * envelope[None, :, None, None]).astype(jnp.float32)


def draw_atom_plane(key, part):
    key = jax.random.fold_in(key, 23)
    plane_key, order_key = jax.random.split(key)
    planes = jax.random.randint(plane_key, (KATOMS,), 0, NX - SPAN + 1, dtype=jnp.int32)
    ranking = jax.random.permutation(order_key, KATOMS)
    planes = planes.at[ranking[0]].set(0)
    return planes.at[ranking[1]].set(NX - SPAN)


def block_scale(key, dims, shards, least, largest):
    factor_of, own = 1.0, jax.random.fold_in(key, 6)
    for axis_at, shards_of in shards:
        steps = jnp.exp(jax.random.uniform(jax.random.fold_in(own, axis_at), (shards_of,), jnp.float32, least / len(shards), largest / len(shards)))
        factor_of = factor_of * jnp.repeat(steps, dims[axis_at] // shards_of).reshape([-1 if axis == axis_at else 1 for axis in range(len(dims))])
    return factor_of


def setup_inputs(seed: int = 0) -> dict:
    seeds = jax.random.split(jax.random.key(seed), 8)
    return {
        "band_orbitals": draw_band_orbitals(jax.random.fold_in(seeds[7], 71), 0),
        "local_potential": jnp.clip(jnp.exp(math.log(2.0) - 2.3025851 * jax.random.uniform(seeds[1], (NX, NY, NZ), jnp.float32) ** block_scale(seeds[1], (NX, NY, NZ), ((0, 64),), -0.2, 0.2)), 0.2, 2.0),
        "band_shift": jnp.clip(jnp.exp(jax.random.uniform(seeds[2], (NB,), jnp.float32, math.log(0.1), math.log(1.0))), 0.1, 1.0),
        "trial_potentials": jnp.clip(-0.5 + 2.5 * jax.random.uniform(seeds[3], (POTS, NX, NY, NZ), jnp.float32) ** block_scale(seeds[3], (POTS, NX, NY, NZ), ((0, 4), (1, 64)), -0.2, 0.2), -0.5, 2.0),
        "projector_blocks": jnp.clip(jax.random.uniform(seeds[4], (KATOMS, SPAN, NY, NZ), jnp.float32, 0.2, 1.8), 0.2, 1.8),
        "atom_plane": draw_atom_plane(jax.random.fold_in(seeds[7], 71), 0),
        "projector_weight": jnp.clip(jnp.exp(jax.random.uniform(seeds[6], (KATOMS,), jnp.float32, math.log(0.5), math.log(4.0))), 0.5, 4.0),
    }


NEAR_COEF = 4.0 / 3.0
FAR_COEF = -1.0 / 12.0
SELF_COEF = -2.5
HIGHEST = lax.Precision.HIGHEST


def kinetic(field):
    total = 3.0 * SELF_COEF * field
    for axis_num in (1, 2, 3):
        total = total + FAR_COEF * (jnp.roll(field, 2, axis_num) + jnp.roll(field, -2, axis_num)) + NEAR_COEF * (jnp.roll(field, 1, axis_num) + jnp.roll(field, -1, axis_num))
    return -0.5 * total


def apply_operator(field, band_orbitals, local_potential, band_shift, projector_blocks, atom_plane, projector_weight):
    cell_count = NX * NY * NZ
    result = kinetic(field) + (local_potential[None] + band_shift[:, None, None, None]) * field
    correlation = jnp.einsum("nxyz,mxyz->nm", field, band_orbitals, precision=HIGHEST) / cell_count
    result = result + jnp.einsum("nm,mxyz->nxyz", correlation, band_orbitals, precision=HIGHEST)
    for atom_idx in range(KATOMS):
        begin = atom_plane[atom_idx]
        window = lax.dynamic_slice_in_dim(field, begin, SPAN, 1)
        amount = jnp.sum(window * projector_blocks[atom_idx][None], axis=(1, 2, 3)) / (SPAN * NY * NZ)
        added = projector_weight[atom_idx] * amount[:, None, None, None] * projector_blocks[atom_idx][None]
        current = lax.dynamic_slice_in_dim(result, begin, SPAN, 1)
        result = lax.dynamic_update_slice_in_dim(result, current + added, begin, 1)
    return result


def reference(band_orbitals, local_potential, band_shift, trial_potentials, projector_blocks, atom_plane, projector_weight):
    cell_count = NX * NY * NZ

    def inner(left, right):
        return jnp.sum(left * right, axis=(1, 2, 3)) / cell_count

    def solve_one(potential):
        source = -potential[None] * band_orbitals
        solution = jnp.zeros_like(source)
        residual = source
        direction = source
        norm_now = inner(residual, residual)
        for sweep in range(ITERS):
            op_image = apply_operator(direction, band_orbitals, local_potential, band_shift, projector_blocks, atom_plane, projector_weight)
            step_len = norm_now / inner(direction, op_image)
            solution = solution + step_len[:, None, None, None] * direction
            if sweep + 1 < ITERS:
                residual = residual - step_len[:, None, None, None] * op_image
                norm_next = inner(residual, residual)
                direction = residual + (norm_next / norm_now)[:, None, None, None] * direction
                norm_now = norm_next
        density = 2.0 * jnp.sum(band_orbitals * solution, axis=0)
        row = jnp.tensordot(trial_potentials, density, axes=((1, 2, 3), (0, 1, 2)), precision=HIGHEST) / cell_count
        return solution, row

    solution, response = lax.map(solve_one, trial_potentials)
    return solution, response
```

```python
import jax
import jax.numpy as jnp
from jax import lax
from jax.experimental import pallas as pl
from jax.experimental.pallas import tpu as pltpu
from jax.sharding import PartitionSpec as P

MESH = pl.DeviceIdType.MESH
F32 = jnp.float32
DOMS, POTS_AXIS = 64, 4
NB, ATOMS, LOC = 4, 8, 2
PAIRS = LOC * NB
NY, NZ, HALF = 192, 128, 96
BLK = 24
KU = ATOMS + NB
CELLS = 128 * 192 * 128
BLOCK_CELLS = 2 * 192 * 128
C1P, C1V, C2P, C2V, C3P, C3V = 0, 2, 4, 6, 8, 10
BCAST = 12
VG = BCAST + 18
ROWS = VG + 3
NSEM = ROWS + 3


def kernel(
    psi_h, lp_h, v_h, proj_h, shift_s, plane_s, weight_s,
    sol_h, resp_o,
    psi, v, lp, proj, vall, stg, ph1, ph2, ph3, vh1, vh2, vh3,
    bb, yb, pj, sol, acc, ct, rowb, slots, lsem, ss, rs, gate,
):
    dom, pot = lax.axis_index("dom"), lax.axis_index("pot")
    right, left = (dom + 1) % DOMS, (dom + DOMS - 1) % DOMS
    mate, part = (pot // 2) * 2 + 1 - pot % 2, (pot + 2) % 4
    plane_xy, zc = dom // 8, dom % 8

    loads = [
        (psi_h.at[pot, :, pl.ds(0, HALF)], stg.at[0, :, pl.ds(0, HALF)]),
        (lp_h.at[:, pl.ds(24 * pot, 24)], stg.at[0, :, pl.ds(HALF, 24)]),
        (psi_h.at[pot, :, pl.ds(HALF, HALF)], stg.at[1, :, pl.ds(0, HALF)]),
        (lp_h.at[:, pl.ds(HALF + 24 * pot, 24)], stg.at[1, :, pl.ds(HALF, 24)]),
        (v_h, v),
        (psi_h, psi),
        (lp_h, lp),
        (proj_h, proj),
    ]
    loads = [pltpu.make_async_copy(a, b, lsem.at[i]) for i, (a, b) in enumerate(loads)]
    for c in loads:
        c.start()

    bar = pltpu.get_barrier_semaphore()

    def greet(d, p):
        pl.semaphore_signal(bar, inc=1, device_id=(d, p), device_id_type=MESH)

    greet(right, pot)
    greet(left, pot)
    greet(dom, mate)
    greet(dom, part)
    for k in range(1, 8):
        greet(plane_xy * 8 + (zc + k) % 8, pot)
        greet(((plane_xy + k) % 8) * 8 + zc, pot)
    for c in loads[:5]:
        c.wait()
    pl.semaphore_wait(bar, 18)

    def remote(i, src, dst, device):
        return pltpu.make_async_remote_copy(
            src, dst, ss.at[i], rs.at[i], device_id=device, device_id_type=MESH
        )

    low, high = pl.ds(0, HALF), pl.ds(HALF, HALF)
    to = ((right, pot), (left, pot))
    near, far = (low, high), (high, low)
    c1p = [remote(C1P + s, stg.at[s], ph1.at[s, pot], to[s]) for s in (0, 1)]
    c1v = [remote(C1V + s, v.at[:, :, near[s]], vh1.at[s], to[s]) for s in (0, 1)]
    c2p = [remote(C2P + s, psi.at[pot, :, far[s]], ph2.at[s, pot], to[s]) for s in (0, 1)]
    c2v = [remote(C2V + s, v.at[:, :, far[s]], vh2.at[s], to[s]) for s in (0, 1)]
    c3p = [remote(C3P + s, ph1.at[s, pot, :, low], ph3.at[s, pot], to[s]) for s in (0, 1)]
    c3v = [remote(C3V + s, vh1.at[s], vh3.at[s], to[s]) for s in (0, 1)]

    def spread(ch, s):
        ref = (ph1, ph2, ph3)[ch]
        i = BCAST + ch * 6 + s * 3
        own, other = ref.at[s, pot], ref.at[s, part]
        return (
            remote(i, own, own, (dom, mate)),
            remote(i + 1, own, own, (dom, part)),
            remote(i + 2, other, other, (dom, mate)),
        )

    spreads = [[spread(ch, s) for s in (0, 1)] for ch in range(3)]
    vown, vpart = vall.at[pl.ds(2 * pot, 2)], vall.at[pl.ds(2 * part, 2)]
    vg = (
        remote(VG, v, vown, (dom, mate)),
        remote(VG + 1, v, vown, (dom, part)),
        remote(VG + 2, vpart, vpart, (dom, mate)),
    )

    def start(copies):
        for c in copies:
            c.start()

    def arrive(copies):
        for c in copies:
            c.wait_recv()

    def pass_on(ch, copies):
        arrive(copies)
        for s in (0, 1):
            spreads[ch][s][1].start()
        for s in (0, 1):
            spreads[ch][s][0].start()

    def pass_mate(ch):
        for s in (0, 1):
            spreads[ch][s][1].wait_recv()
            spreads[ch][s][2].start()

    def gathered(ch):
        for s in (0, 1):
            spreads[ch][s][0].wait_recv()
            spreads[ch][s][2].wait_recv()

    start(c1p)
    start(c1v)
    for k in range(1, 8):
        pl.semaphore_signal(
            gate, inc=1, device_id=(((plane_xy + k) % 8) * 8 + zc, pot), device_id_type=MESH
        )
    loads[5].wait()
    start(c2p)
    start(c2v)

    acc[...] = jnp.zeros_like(acc)
    lane = lax.broadcasted_iota(jnp.int32, (8, NZ), 1)
    wvec = jnp.where((lane >= ATOMS) & (lane < KU), 1.0 / CELLS, 0.0)
    for a in range(ATOMS):
        wvec = jnp.where(lane == a, weight_s[a] / BLOCK_CELLS, wvec)

    def loop(n, body):
        def step(i, _):
            body(i)
            return 0

        lax.fori_loop(0, n, step, 0)

    def rows(j, base=0):
        return pl.multiple_of(base + j * BLK, 8)

    def products(j, base, planes, vref, vrows, pref, prows):
        at = pl.ds(rows(j, base + 8), BLK)
        for w in (0, 1):
            pots = [vref(p, w, pl.ds(rows(j, vrows), BLK)) for p in range(LOC)]
            for n in range(NB):
                orb = pref(n, w, pl.ds(rows(j, prows), BLK))
                for p in range(LOC):
                    bb[p * NB + n, planes + w, at, :] = pots[p] * orb

    def wrap(planes):
        for i in range(PAIRS):
            for k in planes:
                bb[i, k, pl.ds(200, 8), :] = bb[i, k, pl.ds(8, 8), :]
                bb[i, k, pl.ds(0, 8), :] = bb[i, k, pl.ds(192, 8), :]

    loop(8, lambda j: products(j, 0, 4, lambda p, w, r: v[p, w, r, :], 0, lambda n, w, r: psi[n, w, r, :], 0))
    wrap((4, 5))

    loads[6].wait()
    loads[7].wait()

    def project(a):
        first = plane_s[a]
        pick = []
        for k in range(6):
            x = (2 * dom + k - 2 + 128) % 128
            pick.append([jnp.where(first + w == x, 1.0, 0.0) for w in (0, 1)])

        def block(j):
            for base, ks in ((0, (0, 1, 2, 3)), (HALF, (2, 3, 4, 5))):
                at = pl.ds(rows(j, base), BLK)
                p0, p1 = proj[a, 0, at, :], proj[a, 1, at, :]
                for k in ks:
                    pj[a, k, at, :] = pick[k][0] * p0 + pick[k][1] * p1

        loop(4, block)

    loop(ATOMS, project)

    def put(i, k, value):
        acc[pl.ds(pl.multiple_of(((PAIRS - i) % PAIRS * 16 + k) * 8, 8), 8), :] = value

    def get(i, k):
        return acc[pl.ds(pl.multiple_of(((PAIRS - i) % PAIRS * 16 + k) * 8, 8), 8), :]

    zero = jnp.zeros((8, NZ), F32)

    def own_fields(w, at):
        return [pj[a, 2 + w, at, :] for a in range(ATOMS)] + [psi[m, w, at, :] for m in range(NB)]

    def amounts(i):
        def step(j, sums):
            sums = list(sums)
            for w in (0, 1):
                for t in range(BLK // 8):
                    r = pl.multiple_of(j * BLK + 8 * t, 8)
                    x = bb[i, 4 + w, pl.ds(r + 8, 8), :]
                    for k, u in enumerate(own_fields(w, pl.ds(r, 8))):
                        sums[k] += u * x
                    sums[KU] += x * x
            return tuple(sums)

        sums = lax.fori_loop(0, 8, step, (zero,) * (KU + 1))
        for k in range(KU + 1):
            put(i, k, sums[k])

    def form_own(i):
        shift = shift_s[i % NB] + 3.75

        def step(j, total):
            for t in range(BLK // 8):
                r = pl.multiple_of(j * BLK + 8 * t, 8)
                xs = []
                for w in (0, 1):
                    x = bb[i, 4 + w, pl.ds(r + 8, 8), :]
                    s1 = bb[i, 4 + w, pl.ds(r + 9, 8), :] + pltpu.roll(x, NZ - 1, 1)
                    s2 = bb[i, 4 + w, pl.ds(r + 10, 8), :] + pltpu.roll(x, NZ - 2, 1)
                    total += x * ((lp[w, pl.ds(r, 8), :] + shift) * x - (4.0 / 3.0) * s1 + (1.0 / 12.0) * s2)
                    xs.append(x)
                total -= (4.0 / 3.0) * xs[0] * xs[1]
            return total

        return lax.fori_loop(0, 8, step, zero)

    def form_cross(i):
        def step(j, total):
            for t in range(BLK // 8):
                r = pl.multiple_of(j * BLK + 8 * t, 8)
                x2, x3, x4, x5 = [bb[i, k, pl.ds(r + 8, 8), :] for k in (2, 3, 4, 5)]
                total += x4 * ((1.0 / 12.0) * x2 - (4.0 / 3.0) * x3) + (1.0 / 12.0) * (x3 * x5)
                x4, x5, x6, x7 = [bb[i, k, pl.ds(r + 8 + HALF, 8), :] for k in (4, 5, 6, 7)]
                total += x5 * ((1.0 / 12.0) * x7 - (4.0 / 3.0) * x6) + (1.0 / 12.0) * (x4 * x6)
            return total

        return lax.fori_loop(0, 4, step, zero)

    def send_row(t):
        parts = acc[pl.ds(0, 128, stride=8), :]
        for s in range(1, 8):
            parts += acc[pl.ds(s, 128, stride=8), :]
        row = lax.dot_general(
            jnp.ones((8, NZ), F32), parts, (((1,), (1,)), ((), ())),
            precision=lax.Precision.HIGHEST, preferred_element_type=F32,
        )
        rowb[t] = row
        slots[t, pl.ds(dom, 1), :] = row[0:1]

        def one(e, _):
            xj, yj, zj = e // 16, (e // 8) % 2, e % 8
            dx = jnp.where(xj % 2 == 1, 2 - (xj + 1) // 2, 2 + xj // 2)
            dz = jnp.where(zj % 2 == 1, 4 - (zj + 1) // 2, 4 + zj // 2)
            dy = 1 - yj
            peer = ((dom // 16 + dx) % 4) * 16 + ((dom // 8 + dy) % 2) * 8 + (dom + dz) % 8
            remote(ROWS + t, rowb.at[t, pl.ds(0, 1)], slots.at[t, pl.ds(dom, 1)], (peer, pot)).start()
            return 0

        lax.fori_loop(0, DOMS - 1, one, 0)

    def rows_copy(t):
        return remote(ROWS + t, slots.at[t, pl.ds(0, DOMS - 1)], slots.at[t, pl.ds(0, DOMS - 1)], (right, pot))

    def take_row(t):
        rows_copy(t).wait_recv()
        total = jnp.sum(slots[t], axis=0, keepdims=True)
        return pltpu.roll(jnp.broadcast_to(total, (8, NZ)), 0, 1, stride=16, stride_axis=0)

    def column(m, k):
        return jnp.sum(jnp.where(lane == k, m, 0.0), axis=1, keepdims=True)

    pass_on(0, c1p)
    start(c3p)
    loop(PAIRS, amounts)
    pass_mate(0)
    loop(PAIRS, lambda i: put(i, KU + 1, form_own(i)))
    arrive(c1v)
    start(c3v)
    gathered(0)
    for s, base, planes in ((0, 0, 2), (1, HALF, 6)):
        loop(4, lambda j: products(j, base, planes, lambda p, w, r: vh1[s, p, w, r, :], 0, lambda n, w, r: ph1[s, n, w, r, :], 0))
    loop(PAIRS, lambda i: put(i, KU + 1, get(i, KU + 1) + form_cross(i)))
    pl.semaphore_wait(gate, 7)
    send_row(0)

    pass_on(1, c2p)
    pass_mate(1)
    start(vg[:2])
    arrive(c2v)
    gathered(1)
    for s, base, planes in ((0, HALF, 2), (1, 0, 6)):
        loop(4, lambda j: products(j, base, planes, lambda p, w, r: vh2[s, p, w, r, :], 0, lambda n, w, r: ph2[s, n, w, r, :], 0))
    wrap((2, 3, 6, 7))

    def local(i, k, r, lpv):
        def at(dk, dr):
            return bb[i, k + dk, pl.ds(r + 8 + dr, BLK), :]

        x = at(0, 0)
        s1 = at(-1, 0) + at(1, 0) + at(0, -1) + at(0, 1) + pltpu.roll(x, 1, 1) + pltpu.roll(x, NZ - 1, 1)
        s2 = at(-2, 0) + at(2, 0) + at(0, -2) + at(0, 2) + pltpu.roll(x, 2, 1) + pltpu.roll(x, NZ - 2, 1)
        yb[i, k - 2, pl.ds(r, BLK), :] = lpv * x - (2.0 / 3.0) * s1 + (1.0 / 24.0) * s2

    def local_own(i):
        shift = shift_s[i % NB] + 3.75

        def block(j):
            r = rows(j)
            for w in (0, 1):
                local(i, 4 + w, r, lp[w, pl.ds(r, BLK), :] + shift)

        loop(8, block)

    loop(PAIRS, local_own)

    pass_on(2, c3p)
    pass_mate(2)
    arrive(c3v)
    gathered(2)
    for s, base, planes in ((0, 0, 0), (1, HALF, 8)):
        loop(4, lambda j: products(j, base, planes, lambda p, w, r: vh3[s, p, w, r, :], 0, lambda n, w, r: ph3[s, n, w, r, :], 0))

    def local_beside(i):
        shift = shift_s[i % NB] + 3.75

        def block(j):
            for s, base, planes in ((0, 0, 2), (1, HALF, 6)):
                r = rows(j, base)
                for w in (0, 1):
                    local(i, planes + w, r, ph1[s, j, w, pl.ds(HALF, 24), :] + shift)

        loop(4, block)

    loop(PAIRS, local_beside)

    m1 = take_row(0)
    rr0 = column(m1, KU)
    alpha0 = rr0 / (column(m1, KU + 1) + jnp.sum(wvec * m1 * m1, axis=1, keepdims=True))
    coef = alpha0 * wvec * m1
    for k in range(KU):
        ct[k] = jnp.broadcast_to(column(coef, k), (8, NZ))
    ct[KU] = jnp.broadcast_to(alpha0, (8, NZ))

    def residual(i):
        scale = [ct[k, pl.ds(i, 1), :] for k in range(KU + 1)]

        def reduced(k, r, fields):
            x = bb[i, k, pl.ds(r + 8, 8), :] - scale[KU] * yb[i, k - 2, pl.ds(r, 8), :]
            y = scale[0] * fields[0]
            for c, u in zip(scale[1:KU], fields[1:]):
                y += c * u
            x = x - y
            bb[i, k, pl.ds(r + 8, 8), :] = x
            return x

        def step(j, sums):
            sums = list(sums)
            for w in (0, 1):
                for t in range(BLK // 8):
                    r = pl.multiple_of(j * BLK + 8 * t, 8)
                    fields = own_fields(w, pl.ds(r, 8))
                    x = reduced(4 + w, r, fields)
                    for k, u in enumerate(fields):
                        sums[k] += u * x
                    sums[KU] += x * x
            return tuple(sums)

        sums = lax.fori_loop(0, 8, step, (zero,) * (KU + 1))
        for k in range(KU + 1):
            put(i, k, sums[k])

        def beside(j):
            for s, base, planes in ((0, 0, 2), (1, HALF, 6)):
                for w in (0, 1):
                    for t in range(BLK // 8):
                        r0 = pl.multiple_of(j * BLK + 8 * t, 8)
                        at = pl.ds(r0 + base, 8)
                        fields = [pj[a, planes - 2 + w, at, :] for a in range(ATOMS)]
                        fields += [ph1[s, m, w, pl.ds(r0, 8), :] for m in range(NB)]
                        reduced(planes + w, r0 + base, fields)

        loop(4, beside)
        for k in (4, 5):
            bb[i, k, pl.ds(200, 8), :] = bb[i, k, pl.ds(8, 8), :]
        put(i, KU + 1, form_own(i) + form_cross(i))

    loop(PAIRS, residual)
    send_row(1)

    vg[1].wait_recv()
    vg[2].start()
    vg[0].wait_recv()
    vg[2].wait_recv()
    vall[pl.ds(2 * pot, 2)] = v[...]

    def response(i):
        p, n = i // NB, i % NB

        def step(j, sums):
            sums = list(sums)
            for w in (0, 1):
                for t in range(BLK // 8):
                    r = pl.multiple_of(j * BLK + 8 * t, 8)
                    at = pl.ds(r, 8)
                    orb = psi[n, w, at, :]
                    f0 = orb * (orb * v[p, w, at, :])
                    f1 = orb * bb[i, 4 + w, pl.ds(r + 8, 8), :]
                    for q in range(8):
                        u = vall[q, w, at, :]
                        sums[q] += u * f0
                        sums[8 + q] += u * f1
            return tuple(sums)

        sums = lax.fori_loop(0, 8, step, (zero,) * 16)
        for k in range(16):
            put(i, k, sums[k])

    loop(PAIRS, response)
    send_row(2)

    m2 = take_row(1)
    rr1 = column(m2, KU)
    curve = column(m2, KU + 1) + jnp.sum(wvec * m2 * m2, axis=1, keepdims=True)
    alpha1 = rr1 / (curve - rr1 * (rr1 / rr0) / alpha0)
    first = alpha0 + alpha1 * (rr1 / rr0)
    ct[0] = jnp.broadcast_to(-first, (8, NZ))
    ct[1] = jnp.broadcast_to(-alpha1, (8, NZ))

    def write(i):
        p, n = i // NB, i % NB
        one, two = ct[0, pl.ds(i, 1), :], ct[1, pl.ds(i, 1), :]

        def block(j):
            r = rows(j)
            for w in (0, 1):
                at = pl.ds(r, BLK)
                sol[p, n, w, at, :] = one * (v[p, w, at, :] * psi[n, w, at, :]) + two * bb[i, 4 + w, pl.ds(r + 8, BLK), :]

        loop(8, block)

    loop(PAIRS, write)
    out = pltpu.make_async_copy(sol, sol_h, lsem.at[8])
    out.start()

    m3 = take_row(2)
    each = (-2.0 / CELLS) * (first * m3 + alpha1 * pltpu.roll(m3, NZ - 8, 1))
    for p in range(LOC):
        resp_o[p : p + 1, :] = jnp.sum(each[p * NB : (p + 1) * NB, :8], axis=0, keepdims=True)

    out.wait()
    for c in c1p + c1v + c2p + c2v + c3p + c3v + list(vg):
        c.wait_send()
    for ch in spreads:
        for s in ch:
            for c in s:
                c.wait_send()
    for t in range(3):
        rows_copy(t).wait_send()


def shards(band_orbitals, local_potential, band_shift, trial_potentials, projector_blocks, atom_plane, projector_weight):
    anyspec = pl.BlockSpec(memory_space=pl.ANY)
    smem = pl.BlockSpec(memory_space=pltpu.SMEM)
    vm = lambda *shape: pltpu.VMEM(shape, F32)
    return pl.pallas_call(
        kernel,
        out_shape=(
            jax.ShapeDtypeStruct((LOC, NB, 2, NY, NZ), F32),
            jax.ShapeDtypeStruct((LOC, 8), F32),
        ),
        in_specs=[anyspec] * 4 + [smem] * 3,
        out_specs=(anyspec, pl.BlockSpec(memory_space=pltpu.VMEM)),
        scratch_shapes=[
            vm(NB, 2, NY, NZ),
            vm(LOC, 2, NY, NZ),
            vm(2, NY, NZ),
            vm(ATOMS, 2, NY, NZ),
            vm(8, 2, NY, NZ),
            vm(2, 2, HALF + 24, NZ),
            vm(2, NB, 2, HALF + 24, NZ),
            vm(2, NB, 2, HALF, NZ),
            vm(2, NB, 2, HALF, NZ),
            vm(2, LOC, 2, HALF, NZ),
            vm(2, LOC, 2, HALF, NZ),
            vm(2, LOC, 2, HALF, NZ),
            vm(PAIRS, 10, NY + 16, NZ),
            vm(PAIRS, 6, NY, NZ),
            vm(ATOMS, 6, NY, NZ),
            vm(LOC, NB, 2, NY, NZ),
            vm(1024, NZ),
            vm(KU + 1, 8, NZ),
            vm(3, 8, NZ),
            vm(3, DOMS, NZ),
            pltpu.SemaphoreType.DMA((9,)),
            pltpu.SemaphoreType.DMA((NSEM,)),
            pltpu.SemaphoreType.DMA((NSEM,)),
            pltpu.SemaphoreType.REGULAR,
        ],
        compiler_params=pltpu.CompilerParams(
            collective_id=0, has_side_effects=True, vmem_limit_bytes=48 * 2**20
        ),
    )(band_orbitals, local_potential, trial_potentials, projector_blocks, band_shift, atom_plane, projector_weight)


def solution(mesh):
    placed = (
        P(None, "dom", None, None),
        P("dom", None, None),
        P(),
        P("pot", "dom", None, None),
        P(),
        P(),
        P(),
    )
    return jax.shard_map(
        shards,
        mesh=mesh,
        in_specs=placed,
        out_specs=(P("pot", None, "dom", None, None), P("pot", None)),
        check_vma=False,
    )
```

```python
import jax
import jax.numpy as jnp
from jax import lax
from jax.experimental import pallas as pl
from jax.experimental.pallas import tpu as pltpu
from jax.sharding import PartitionSpec as P

MESH = pl.DeviceIdType.MESH
F32 = jnp.float32
DOMS, POTS_AXIS = 64, 4
NB, ATOMS, LOC = 4, 8, 2
PAIRS = LOC * NB
NY, NZ, HALF = 192, 128, 96
BLK = 24
KU = ATOMS + NB
CELLS = 128 * 192 * 128
BLOCK_CELLS = 2 * 192 * 128
C1P, C1V, C2P, C2V, C3P, C3V = 0, 2, 4, 6, 8, 10
BCAST = 12
VG = BCAST + 6
ROWS = VG + 3
NSEM = ROWS + 3


def kernel(
    psi_h, lp_h, v_h, proj_h, shift_s, plane_s, weight_s,
    sol_h, resp_o,
    psi, v, lp, proj, vall, stg, ph1, ph2, ph3, vh1, vh2, vh3,
    bb, yb, pj, sol, acc, ct, rowb, slots, lsem, ss, rs, gate,
):
    dom, pot = lax.axis_index("dom"), lax.axis_index("pot")
    right, left = (dom + 1) % DOMS, (dom + DOMS - 1) % DOMS
    mate, part = (pot // 2) * 2 + 1 - pot % 2, (pot + 2) % 4
    plane_xy, zc = dom // 8, dom % 8

    core = pot % 2
    mine = pl.ds(2 * core, 2)
    loads = []
    for s in (0, 1):
        loads.append((psi_h.at[mine, :, pl.ds(s * HALF, HALF)], stg.at[s, :, :, pl.ds(0, HALF)]))
        for b in (0, 1):
            quarter = pl.ds(s * HALF + 24 * (2 * core + b), 24)
            loads.append((lp_h.at[:, quarter], stg.at[s, b, :, pl.ds(HALF, 24)]))
    loads += [
        (v_h, v),
        (psi_h, psi),
        (lp_h, lp),
        (proj_h, proj),
    ]
    loads = [pltpu.make_async_copy(a, b, lsem.at[i]) for i, (a, b) in enumerate(loads)]
    for c in loads:
        c.start()

    bar = pltpu.get_barrier_semaphore()

    def greet(d, p):
        pl.semaphore_signal(bar, inc=1, device_id=(d, p), device_id_type=MESH)

    greet(right, pot)
    greet(left, pot)
    greet(dom, mate)
    greet(dom, part)
    for k in range(1, 8):
        greet(plane_xy * 8 + (zc + k) % 8, pot)
        greet(((plane_xy + k) % 8) * 8 + zc, pot)
    for c in loads[:7]:
        c.wait()
    pl.semaphore_wait(bar, 18)

    def remote(i, src, dst, device):
        return pltpu.make_async_remote_copy(
            src, dst, ss.at[i], rs.at[i], device_id=device, device_id_type=MESH
        )

    low, high = pl.ds(0, HALF), pl.ds(HALF, HALF)
    to = ((right, pot), (left, pot))
    near, far = (low, high), (high, low)
    c1p = [remote(C1P + s, stg.at[s], ph1.at[s, mine], to[s]) for s in (0, 1)]
    c1v = [remote(C1V + s, v.at[:, :, near[s]], vh1.at[s], to[s]) for s in (0, 1)]
    c2p = [remote(C2P + s, psi.at[mine, :, far[s]], ph2.at[s, mine], to[s]) for s in (0, 1)]
    c2v = [remote(C2V + s, v.at[:, :, far[s]], vh2.at[s], to[s]) for s in (0, 1)]
    c3p = [remote(C3P + s, ph1.at[s, mine, :, low], ph3.at[s, mine], to[s]) for s in (0, 1)]
    c3v = [remote(C3V + s, vh1.at[s], vh3.at[s], to[s]) for s in (0, 1)]

    def spread(ch, s):
        own = (ph1, ph2, ph3)[ch].at[s, mine]
        return remote(BCAST + ch * 2 + s, own, own, (dom, mate))

    spreads = [[spread(ch, s) for s in (0, 1)] for ch in range(3)]
    vown, vpart = vall.at[pl.ds(2 * pot, 2)], vall.at[pl.ds(2 * part, 2)]
    vg = (
        remote(VG, v, vown, (dom, mate)),
        remote(VG + 1, v, vown, (dom, part)),
        remote(VG + 2, vpart, vpart, (dom, mate)),
    )

    def start(copies):
        for c in copies:
            c.start()

    def arrive(copies):
        for c in copies:
            c.wait_recv()

    def pass_on(ch, copies):
        arrive(copies)
        start(spreads[ch])

    start(c1p)
    start(c1v)
    for k in range(1, 8):
        pl.semaphore_signal(
            gate, inc=1, device_id=(((plane_xy + k) % 8) * 8 + zc, pot), device_id_type=MESH
        )
    loads[7].wait()
    start(c2p)
    start(c2v)

    acc[...] = jnp.zeros_like(acc)
    lane = lax.broadcasted_iota(jnp.int32, (8, NZ), 1)
    wvec = jnp.where((lane >= ATOMS) & (lane < KU), 1.0 / CELLS, 0.0)
    for a in range(ATOMS):
        wvec = jnp.where(lane == a, weight_s[a] / BLOCK_CELLS, wvec)

    def loop(n, body):
        def step(i, _):
            body(i)
            return 0

        lax.fori_loop(0, n, step, 0)

    def rows(j, base=0):
        return pl.multiple_of(base + j * BLK, 8)

    def products(j, base, planes, vref, vrows, pref, prows):
        at = pl.ds(rows(j, base + 8), BLK)
        for w in (0, 1):
            pots = [vref(p, w, pl.ds(rows(j, vrows), BLK)) for p in range(LOC)]
            for n in range(NB):
                orb = pref(n, w, pl.ds(rows(j, prows), BLK))
                for p in range(LOC):
                    bb[p * NB + n, planes + w, at, :] = pots[p] * orb

    def wrap(planes):
        for i in range(PAIRS):
            for k in planes:
                bb[i, k, pl.ds(200, 8), :] = bb[i, k, pl.ds(8, 8), :]
                bb[i, k, pl.ds(0, 8), :] = bb[i, k, pl.ds(192, 8), :]

    loop(8, lambda j: products(j, 0, 4, lambda p, w, r: v[p, w, r, :], 0, lambda n, w, r: psi[n, w, r, :], 0))
    wrap((4, 5))

    loads[8].wait()
    loads[9].wait()

    def project(a):
        first = plane_s[a]
        pick = []
        for k in range(6):
            x = (2 * dom + k - 2 + 128) % 128
            pick.append([jnp.where(first + w == x, 1.0, 0.0) for w in (0, 1)])

        def block(j):
            for base, ks in ((0, (0, 1, 2, 3)), (HALF, (2, 3, 4, 5))):
                at = pl.ds(rows(j, base), BLK)
                p0, p1 = proj[a, 0, at, :], proj[a, 1, at, :]
                for k in ks:
                    pj[a, k, at, :] = pick[k][0] * p0 + pick[k][1] * p1

        loop(4, block)

    loop(ATOMS, project)

    def put(i, k, value):
        acc[pl.ds(pl.multiple_of(((PAIRS - i) % PAIRS * 16 + k) * 8, 8), 8), :] = value

    def get(i, k):
        return acc[pl.ds(pl.multiple_of(((PAIRS - i) % PAIRS * 16 + k) * 8, 8), 8), :]

    zero = jnp.zeros((8, NZ), F32)

    def own_fields(w, at):
        return [pj[a, 2 + w, at, :] for a in range(ATOMS)] + [psi[m, w, at, :] for m in range(NB)]

    def amounts(i):
        def step(j, sums):
            sums = list(sums)
            for w in (0, 1):
                for t in range(6):
                    r = pl.multiple_of(j * 48 + 8 * t, 8)
                    x = bb[i, 4 + w, pl.ds(r + 8, 8), :]
                    for k, u in enumerate(own_fields(w, pl.ds(r, 8))):
                        sums[k] += u * x
                    sums[KU] += x * x
            return tuple(sums)

        sums = lax.fori_loop(0, 4, step, (zero,) * (KU + 1))
        for k in range(KU + 1):
            put(i, k, sums[k])

    def form_own(i):
        shift = shift_s[i % NB] + 3.75
        total = [zero, zero]
        for r in range(0, NY, 8):
            xs = []
            for w in (0, 1):
                x = bb[i, 4 + w, pl.ds(r + 8, 8), :]
                s1 = bb[i, 4 + w, pl.ds(r + 9, 8), :] + pltpu.roll(x, NZ - 1, 1)
                s2 = bb[i, 4 + w, pl.ds(r + 10, 8), :] + pltpu.roll(x, NZ - 2, 1)
                total[w] += x * ((lp[w, pl.ds(r, 8), :] + shift) * x - (4.0 / 3.0) * s1 + (1.0 / 12.0) * s2)
                xs.append(x)
            total[0] -= (4.0 / 3.0) * xs[0] * xs[1]
        return total[0] + total[1]

    def form_cross(i):
        total = [zero, zero]
        for r in range(0, HALF, 8):
            x2, x3, x4, x5 = [bb[i, k, pl.ds(r + 8, 8), :] for k in (2, 3, 4, 5)]
            total[0] += x4 * ((1.0 / 12.0) * x2 - (4.0 / 3.0) * x3) + (1.0 / 12.0) * (x3 * x5)
            x4, x5, x6, x7 = [bb[i, k, pl.ds(r + 8 + HALF, 8), :] for k in (4, 5, 6, 7)]
            total[1] += x5 * ((1.0 / 12.0) * x7 - (4.0 / 3.0) * x6) + (1.0 / 12.0) * (x4 * x6)
        return total[0] + total[1]

    def send_row(t):
        parts = acc[pl.ds(0, 128, stride=8), :]
        for s in range(1, 8):
            parts += acc[pl.ds(s, 128, stride=8), :]
        row = lax.dot_general(
            jnp.ones((8, NZ), F32), parts, (((1,), (1,)), ((), ())),
            precision=lax.Precision.HIGHEST, preferred_element_type=F32,
        )
        rowb[t] = row
        slots[t, pl.ds(dom, 1), :] = row[0:1]

        def one(e, _):
            xj, yj, zj = e // 16, (e // 8) % 2, e % 8
            dx = jnp.where(xj % 2 == 1, 2 - (xj + 1) // 2, 2 + xj // 2)
            dz = jnp.where(zj % 2 == 1, 4 - (zj + 1) // 2, 4 + zj // 2)
            dy = 1 - yj
            peer = ((dom // 16 + dx) % 4) * 16 + ((dom // 8 + dy) % 2) * 8 + (dom + dz) % 8
            remote(ROWS + t, rowb.at[t, pl.ds(0, 1)], slots.at[t, pl.ds(dom, 1)], (peer, pot)).start()
            return 0

        lax.fori_loop(0, DOMS - 1, one, 0)

    def rows_copy(t):
        return remote(ROWS + t, slots.at[t, pl.ds(0, DOMS - 1)], slots.at[t, pl.ds(0, DOMS - 1)], (right, pot))

    def take_row(t):
        rows_copy(t).wait_recv()
        total = jnp.sum(slots[t], axis=0, keepdims=True)
        return pltpu.roll(jnp.broadcast_to(total, (8, NZ)), 0, 1, stride=16, stride_axis=0)

    def column(m, k):
        return jnp.sum(jnp.where(lane == k, m, 0.0), axis=1, keepdims=True)

    pass_on(0, c1p)
    start(c3p)
    loop(PAIRS, amounts)
    loop(PAIRS, lambda i: put(i, KU + 1, form_own(i)))
    arrive(c1v)
    start(c3v)
    arrive(spreads[0])
    for s, base, planes in ((0, 0, 2), (1, HALF, 6)):
        loop(4, lambda j: products(j, base, planes, lambda p, w, r: vh1[s, p, w, r, :], 0, lambda n, w, r: ph1[s, n, w, r, :], 0))
    loop(PAIRS, lambda i: put(i, KU + 1, get(i, KU + 1) + form_cross(i)))
    pl.semaphore_wait(gate, 7)
    send_row(0)

    pass_on(1, c2p)
    arrive(c2v)
    arrive(spreads[1])
    for s, base, planes in ((0, HALF, 2), (1, 0, 6)):
        loop(4, lambda j: products(j, base, planes, lambda p, w, r: vh2[s, p, w, r, :], 0, lambda n, w, r: ph2[s, n, w, r, :], 0))
    wrap((2, 3, 6, 7))

    def local(i, k, r, lpv):
        def at(dk, dr):
            return bb[i, k + dk, pl.ds(r + 8 + dr, 8), :]

        x = at(0, 0)
        s1 = at(-1, 0) + at(1, 0) + at(0, -1) + at(0, 1) + pltpu.roll(x, 1, 1) + pltpu.roll(x, NZ - 1, 1)
        s2 = at(-2, 0) + at(2, 0) + at(0, -2) + at(0, 2) + pltpu.roll(x, 2, 1) + pltpu.roll(x, NZ - 2, 1)
        yb[i, k - 2, pl.ds(r, 8), :] = lpv * x - (2.0 / 3.0) * s1 + (1.0 / 24.0) * s2

    def local_own(i):
        shift = shift_s[i % NB] + 3.75
        for r in range(0, NY, 8):
            for w in (0, 1):
                local(i, 4 + w, r, lp[w, pl.ds(r, 8), :] + shift)

    loop(PAIRS, local_own)

    pass_on(2, c3p)
    arrive(c3v)
    arrive(spreads[2])
    for s, base, planes in ((0, 0, 0), (1, HALF, 8)):
        loop(4, lambda j: products(j, base, planes, lambda p, w, r: vh3[s, p, w, r, :], 0, lambda n, w, r: ph3[s, n, w, r, :], 0))

    def local_beside(i):
        shift = shift_s[i % NB] + 3.75
        for r in range(0, HALF, 8):
            for s, base, planes in ((0, 0, 2), (1, HALF, 6)):
                for w in (0, 1):
                    lpv = ph1[s, r // 24, w, pl.ds(HALF + r % 24, 8), :]
                    local(i, planes + w, base + r, lpv + shift)

    loop(PAIRS, local_beside)

    m1 = take_row(0)
    start(vg[:2])
    rr0 = column(m1, KU)
    alpha0 = rr0 / (column(m1, KU + 1) + jnp.sum(wvec * m1 * m1, axis=1, keepdims=True))
    coef = alpha0 * wvec * m1
    for k in range(KU):
        ct[k] = jnp.broadcast_to(column(coef, k), (8, NZ))
    ct[KU] = jnp.broadcast_to(alpha0, (8, NZ))

    def residual(i):
        scale = [ct[k, pl.ds(i, 1), :] for k in range(KU + 1)]

        def reduced(k, r, fields):
            x = bb[i, k, pl.ds(r + 8, 8), :] - scale[KU] * yb[i, k - 2, pl.ds(r, 8), :]
            y = scale[0] * fields[0]
            for c, u in zip(scale[1:KU], fields[1:]):
                y += c * u
            x = x - y
            bb[i, k, pl.ds(r + 8, 8), :] = x
            return x

        def step(j, sums):
            sums = list(sums)
            for w in (0, 1):
                for t in range(6):
                    r = pl.multiple_of(j * 48 + 8 * t, 8)
                    fields = own_fields(w, pl.ds(r, 8))
                    x = reduced(4 + w, r, fields)
                    for k, u in enumerate(fields):
                        sums[k] += u * x
                    sums[KU] += x * x
            return tuple(sums)

        sums = lax.fori_loop(0, 4, step, (zero,) * (KU + 1))
        for k in range(KU + 1):
            put(i, k, sums[k])

        def beside(j):
            for s, base, planes in ((0, 0, 2), (1, HALF, 6)):
                for w in (0, 1):
                    for t in range(6):
                        r0 = pl.multiple_of(j * 48 + 8 * t, 8)
                        at = pl.ds(r0 + base, 8)
                        fields = [pj[a, planes - 2 + w, at, :] for a in range(ATOMS)]
                        fields += [ph1[s, m, w, pl.ds(r0, 8), :] for m in range(NB)]
                        reduced(planes + w, r0 + base, fields)

        loop(2, beside)
        for k in (4, 5):
            bb[i, k, pl.ds(200, 8), :] = bb[i, k, pl.ds(8, 8), :]
        put(i, KU + 1, form_own(i) + form_cross(i))

    loop(PAIRS, residual)
    send_row(1)

    vg[1].wait_recv()
    vg[2].start()
    vg[0].wait_recv()
    vg[2].wait_recv()
    vall[pl.ds(2 * pot, 2)] = v[...]

    def response(i):
        p, n = i // NB, i % NB

        def step(j, sums):
            sums = list(sums)
            for w in (0, 1):
                for t in range(6):
                    r = pl.multiple_of(j * 48 + 8 * t, 8)
                    at = pl.ds(r, 8)
                    orb = psi[n, w, at, :]
                    f0 = orb * (orb * v[p, w, at, :])
                    f1 = orb * bb[i, 4 + w, pl.ds(r + 8, 8), :]
                    for q in range(8):
                        u = vall[q, w, at, :]
                        sums[q] += u * f0
                        sums[8 + q] += u * f1
            return tuple(sums)

        sums = lax.fori_loop(0, 4, step, (zero,) * 16)
        for k in range(16):
            put(i, k, sums[k])

    loop(PAIRS, response)
    send_row(2)

    m2 = take_row(1)
    rr1 = column(m2, KU)
    curve = column(m2, KU + 1) + jnp.sum(wvec * m2 * m2, axis=1, keepdims=True)
    alpha1 = rr1 / (curve - rr1 * (rr1 / rr0) / alpha0)
    first = alpha0 + alpha1 * (rr1 / rr0)
    ct[0] = jnp.broadcast_to(-first, (8, NZ))
    ct[1] = jnp.broadcast_to(-alpha1, (8, NZ))

    def write(i):
        p, n = i // NB, i % NB
        one, two = ct[0, pl.ds(i, 1), :], ct[1, pl.ds(i, 1), :]

        def block(j):
            r = rows(j)
            for w in (0, 1):
                at = pl.ds(r, BLK)
                sol[p, n, w, at, :] = one * (v[p, w, at, :] * psi[n, w, at, :]) + two * bb[i, 4 + w, pl.ds(r + 8, BLK), :]

        loop(8, block)

    loop(PAIRS, write)
    out = pltpu.make_async_copy(sol, sol_h, lsem.at[10])
    out.start()

    m3 = take_row(2)
    each = (-2.0 / CELLS) * (first * m3 + alpha1 * pltpu.roll(m3, NZ - 8, 1))
    for p in range(LOC):
        resp_o[p : p + 1, :] = jnp.sum(each[p * NB : (p + 1) * NB, :8], axis=0, keepdims=True)

    out.wait()
    for c in c1p + c1v + c2p + c2v + c3p + c3v + list(vg):
        c.wait_send()
    for ch in spreads:
        for s in ch:
            s.wait_send()
    for t in range(3):
        rows_copy(t).wait_send()


def shards(band_orbitals, local_potential, band_shift, trial_potentials, projector_blocks, atom_plane, projector_weight):
    anyspec = pl.BlockSpec(memory_space=pltpu.HBM)
    smem = pl.BlockSpec(memory_space=pltpu.SMEM)
    vm = lambda *shape: pltpu.VMEM(shape, F32)
    return pl.pallas_call(
        kernel,
        out_shape=(
            jax.ShapeDtypeStruct((LOC, NB, 2, NY, NZ), F32),
            jax.ShapeDtypeStruct((LOC, 8), F32),
        ),
        in_specs=[anyspec] * 4 + [smem] * 3,
        out_specs=(anyspec, pl.BlockSpec(memory_space=pltpu.VMEM)),
        scratch_shapes=[
            vm(NB, 2, NY, NZ),
            vm(LOC, 2, NY, NZ),
            vm(2, NY, NZ),
            vm(ATOMS, 2, NY, NZ),
            vm(8, 2, NY, NZ),
            vm(2, 2, 2, HALF + 24, NZ),
            vm(2, NB, 2, HALF + 24, NZ),
            vm(2, NB, 2, HALF, NZ),
            vm(2, NB, 2, HALF, NZ),
            vm(2, LOC, 2, HALF, NZ),
            vm(2, LOC, 2, HALF, NZ),
            vm(2, LOC, 2, HALF, NZ),
            vm(PAIRS, 10, NY + 16, NZ),
            vm(PAIRS, 6, NY, NZ),
            vm(ATOMS, 6, NY, NZ),
            vm(LOC, NB, 2, NY, NZ),
            vm(1024, NZ),
            vm(KU + 1, 8, NZ),
            vm(3, 8, NZ),
            vm(3, DOMS, NZ),
            pltpu.SemaphoreType.DMA((11,)),
            pltpu.SemaphoreType.DMA((NSEM,)),
            pltpu.SemaphoreType.DMA((NSEM,)),
            pltpu.SemaphoreType.REGULAR,
        ],
        compiler_params=pltpu.CompilerParams(
            collective_id=0, has_side_effects=True, vmem_limit_bytes=63 * 2**20
        ),
    )(band_orbitals, local_potential, trial_potentials, projector_blocks, band_shift, atom_plane, projector_weight)


def solution(mesh):
    placed = (
        P(None, "dom", None, None),
        P("dom", None, None),
        P(),
        P("pot", "dom", None, None),
        P(),
        P(),
        P(),
    )
    return jax.shard_map(
        shards,
        mesh=mesh,
        in_specs=placed,
        out_specs=(P("pot", None, "dom", None, None), P("pot", None)),
        check_vma=False,
    )
```

```python
import jax
import jax.numpy as jnp
from jax import lax
from jax.experimental import pallas as pl
from jax.experimental.pallas import tpu as pltpu
from jax.sharding import PartitionSpec as P

MESH = pl.DeviceIdType.MESH
F32 = jnp.float32
DOMS, POTS_AXIS = 64, 4
NB, ATOMS, LOC = 4, 8, 2
PAIRS = LOC * NB
NY, NZ, HALF = 192, 128, 96
BLK = 24
KU = ATOMS + NB
CELLS = 128 * 192 * 128
BLOCK_CELLS = 2 * 192 * 128
C1P, C1V, C2P, C2V, C3P, C3V = 0, 2, 4, 6, 8, 10
BCAST = 12
VG = BCAST + 6
ROWS = VG + 3
NSEM = ROWS + 3


def kernel(
    psi_h, lp_h, v_h, proj_h, shift_s, plane_s, weight_s,
    sol_h, resp_o,
    psi, v, lp, proj, vall, stg, ph1, ph2, ph3, vh1, vh2, vh3,
    bb, rb, yb, pj, sol, acc, racc, ct, rowb, slots, lsem, ss, rs, gate,
):
    dom, pot = lax.axis_index("dom"), lax.axis_index("pot")
    right, left = (dom + 1) % DOMS, (dom + DOMS - 1) % DOMS
    mate, part = (pot // 2) * 2 + 1 - pot % 2, (pot + 2) % 4
    plane_xy, zc = dom // 8, dom % 8
    ring = [lax.rem(zc + d, 8) for d in (4, 3, 5, 2, 6, 1, 7, 0)]

    core = pot % 2
    mine = pl.ds(2 * core, 2)
    loads = []
    for s in (0, 1):
        loads.append((psi_h.at[mine, :, pl.ds(s * HALF, HALF)], stg.at[s, :, :, pl.ds(0, HALF)]))
        for b in (0, 1):
            quarter = pl.ds(s * HALF + 24 * (2 * core + b), 24)
            loads.append((lp_h.at[:, quarter], stg.at[s, b, :, pl.ds(HALF, 24)]))
    loads += [
        (v_h, v),
        (psi_h, psi),
        (lp_h, lp),
        (proj_h, proj),
    ]
    loads = [pltpu.make_async_copy(a, b, lsem.at[i]) for i, (a, b) in enumerate(loads)]
    for c in loads:
        c.start()

    bar = pltpu.get_barrier_semaphore()

    def greet(d, p):
        pl.semaphore_signal(bar, inc=1, device_id=(d, p), device_id_type=MESH)

    greet(right, pot)
    greet(left, pot)
    greet(dom, mate)
    greet(dom, part)
    for k in range(1, 8):
        greet(plane_xy * 8 + (zc + k) % 8, pot)
        greet(((plane_xy + k) % 8) * 8 + zc, pot)
    for c in loads[:7]:
        c.wait()
    pl.semaphore_wait(bar, 18)

    def remote(i, src, dst, device):
        return pltpu.make_async_remote_copy(
            src, dst, ss.at[i], rs.at[i], device_id=device, device_id_type=MESH
        )

    low, high = pl.ds(0, HALF), pl.ds(HALF, HALF)
    to = ((right, pot), (left, pot))
    near, far = (low, high), (high, low)
    c1p = [remote(C1P + s, stg.at[s], ph1.at[s, mine], to[s]) for s in (0, 1)]
    c1v = [remote(C1V + s, v.at[:, :, near[s]], vh1.at[s], to[s]) for s in (0, 1)]
    c2p = [remote(C2P + s, psi.at[mine, :, far[s]], ph2.at[s, mine], to[s]) for s in (0, 1)]
    c2v = [remote(C2V + s, v.at[:, :, far[s]], vh2.at[s], to[s]) for s in (0, 1)]
    c3p = [remote(C3P + s, ph1.at[s, mine, :, low], ph3.at[s, mine], to[s]) for s in (0, 1)]
    c3v = [remote(C3V + s, vh1.at[s], vh3.at[s], to[s]) for s in (0, 1)]

    def spread(ch, s):
        own = (ph1, ph2, ph3)[ch].at[s, mine]
        return remote(BCAST + ch * 2 + s, own, own, (dom, mate))

    spreads = [[spread(ch, s) for s in (0, 1)] for ch in range(3)]
    vown, vpart = vall.at[pl.ds(2 * pot, 2)], vall.at[pl.ds(2 * part, 2)]
    vg = (
        remote(VG, v, vown, (dom, mate)),
        remote(VG + 1, v, vown, (dom, part)),
        remote(VG + 2, vpart, vpart, (dom, mate)),
    )

    def start(copies):
        for c in copies:
            c.start()

    def arrive(copies):
        for c in copies:
            c.wait_recv()

    def pass_on(ch, copies):
        arrive(copies)
        start(spreads[ch])

    start(c1p)
    start(c1v)
    for k in range(1, 8):
        pl.semaphore_signal(
            gate, inc=1, device_id=(((plane_xy + k) % 8) * 8 + zc, pot), device_id_type=MESH
        )
    loads[7].wait()
    start(c2p)
    start(c2v)

    acc[...] = jnp.zeros_like(acc)
    lane = lax.broadcasted_iota(jnp.int32, (8, NZ), 1)
    wvec = jnp.where((lane >= ATOMS) & (lane < KU), 1.0 / CELLS, 0.0)
    for a in range(ATOMS):
        wvec = jnp.where(lane == a, weight_s[a] / BLOCK_CELLS, wvec)

    def loop(n, body):
        def step(i, _):
            body(i)
            return 0

        lax.fori_loop(0, n, step, 0)

    def rows(j, base=0):
        return pl.multiple_of(base + j * BLK, 8)

    def products(j, base, planes, vref, vrows, pref, prows):
        at = pl.ds(rows(j, base + 8), BLK)
        for w in (0, 1):
            pots = [vref(p, w, pl.ds(rows(j, vrows), BLK)) for p in range(LOC)]
            for n in range(NB):
                orb = pref(n, w, pl.ds(rows(j, prows), BLK))
                for p in range(LOC):
                    bb[p * NB + n, planes + w, at, :] = pots[p] * orb

    def wrap(planes):
        for i in range(PAIRS):
            for k in planes:
                bb[i, k, pl.ds(200, 8), :] = bb[i, k, pl.ds(8, 8), :]
                bb[i, k, pl.ds(0, 8), :] = bb[i, k, pl.ds(192, 8), :]

    loop(8, lambda j: products(j, 0, 4, lambda p, w, r: v[p, w, r, :], 0, lambda n, w, r: psi[n, w, r, :], 0))
    wrap((4, 5))

    loads[8].wait()
    loads[9].wait()

    def project(a):
        first = plane_s[a]
        pick = []
        for k in range(6):
            x = (2 * dom + k - 2 + 128) % 128
            pick.append([jnp.where(first + w == x, 1.0, 0.0) for w in (0, 1)])

        def block(j):
            for base, ks in ((0, (0, 1, 2, 3)), (HALF, (2, 3, 4, 5))):
                at = pl.ds(rows(j, base), BLK)
                p0, p1 = proj[a, 0, at, :], proj[a, 1, at, :]
                for k in ks:
                    pj[a, k, at, :] = pick[k][0] * p0 + pick[k][1] * p1

        loop(4, block)

    loop(ATOMS, project)

    def put(i, k, value, ref=acc):
        ref[pl.ds(pl.multiple_of(((PAIRS - i) % PAIRS * 16 + k) * 8, 8), 8), :] = value

    def get(i, k):
        return acc[pl.ds(pl.multiple_of(((PAIRS - i) % PAIRS * 16 + k) * 8, 8), 8), :]

    zero = jnp.zeros((8, NZ), F32)

    def own_fields(w, at):
        return [pj[a, 2 + w, at, :] for a in range(ATOMS)] + [psi[m, w, at, :] for m in range(NB)]

    def amounts(i):
        def step(j, sums):
            sums = list(sums)
            for w in (0, 1):
                for t in range(6):
                    r = pl.multiple_of(j * 48 + 8 * t, 8)
                    x = bb[i, 4 + w, pl.ds(r + 8, 8), :]
                    for k, u in enumerate(own_fields(w, pl.ds(r, 8))):
                        sums[k] += u * x
                    sums[KU] += x * x
            return tuple(sums)

        sums = lax.fori_loop(0, 4, step, (zero,) * (KU + 1))
        for k in range(KU + 1):
            put(i, k, sums[k])

    def form_own(i, ref, first):
        shift = shift_s[i % NB] + 3.75
        total = [zero, zero]
        for r in range(0, NY, 8):
            xs = []
            for w in (0, 1):
                x = ref[i, first + w, pl.ds(r + 8, 8), :]
                s1 = ref[i, first + w, pl.ds(r + 9, 8), :] + pltpu.roll(x, NZ - 1, 1)
                s2 = ref[i, first + w, pl.ds(r + 10, 8), :] + pltpu.roll(x, NZ - 2, 1)
                total[w] += x * ((lp[w, pl.ds(r, 8), :] + shift) * x - (4.0 / 3.0) * s1 + (1.0 / 12.0) * s2)
                xs.append(x)
            total[0] -= (4.0 / 3.0) * xs[0] * xs[1]
        return total[0] + total[1]

    def form_cross(i, ref, first):
        total = [zero, zero]
        for r in range(0, HALF, 8):
            x2, x3 = [bb[i, k, pl.ds(r + 8, 8), :] for k in (2, 3)]
            x4, x5 = [ref[i, first + w, pl.ds(r + 8, 8), :] for w in (0, 1)]
            total[0] += x4 * ((1.0 / 12.0) * x2 - (4.0 / 3.0) * x3) + (1.0 / 12.0) * (x3 * x5)
            x4, x5 = [ref[i, first + w, pl.ds(r + 8 + HALF, 8), :] for w in (0, 1)]
            x6, x7 = [bb[i, k, pl.ds(r + 8 + HALF, 8), :] for k in (6, 7)]
            total[1] += x5 * ((1.0 / 12.0) * x7 - (4.0 / 3.0) * x6) + (1.0 / 12.0) * (x4 * x6)
        return total[0] + total[1]

    def send_row(t, ref):
        parts = ref[pl.ds(0, 128, stride=8), :]
        for s in range(1, 8):
            parts += ref[pl.ds(s, 128, stride=8), :]
        row = lax.dot_general(
            jnp.ones((8, NZ), F32), parts, (((1,), (1,)), ((), ())),
            precision=lax.Precision.HIGHEST, preferred_element_type=F32,
        )
        rowb[t] = row
        slots[t, pl.ds(dom, 1), :] = row[0:1]

        def give(xy, places):
            for z in places:
                remote(ROWS + t, rowb.at[t, pl.ds(0, 1)], slots.at[t, pl.ds(dom, 1)], (xy * 8 + z, pot)).start()

        def plane(e, _):
            xj, yj = lax.div(e, 2), lax.rem(e, 2)
            dx = jnp.where(xj == 0, 2, jnp.where(xj == 1, 1, 3 - 3 * (xj - 2)))
            x = lax.rem(lax.div(plane_xy, 2) + dx, 4)
            give(x * 2 + lax.rem(plane_xy + 1 - yj, 2), ring)
            return 0

        lax.fori_loop(0, 7, plane, 0)
        give(plane_xy, ring[:7])

    def rows_copy(t):
        return remote(ROWS + t, slots.at[t, pl.ds(0, DOMS - 1)], slots.at[t, pl.ds(0, DOMS - 1)], (right, pot))

    def take_row(t):
        rows_copy(t).wait_recv()
        total = jnp.sum(slots[t], axis=0, keepdims=True)
        return pltpu.roll(jnp.broadcast_to(total, (8, NZ)), 0, 1, stride=16, stride_axis=0)

    def column(m, k):
        return jnp.sum(jnp.where(lane == k, m, 0.0), axis=1, keepdims=True)

    pass_on(0, c1p)
    loop(PAIRS, amounts)
    loop(PAIRS, lambda i: put(i, KU + 1, form_own(i, bb, 4)))
    arrive(c1v)
    arrive(spreads[0])
    for s, base, planes in ((0, 0, 2), (1, HALF, 6)):
        loop(4, lambda j: products(j, base, planes, lambda p, w, r: vh1[s, p, w, r, :], 0, lambda n, w, r: ph1[s, n, w, r, :], 0))
    loop(PAIRS, lambda i: put(i, KU + 1, get(i, KU + 1) + form_cross(i, bb, 4)))
    pl.semaphore_wait(gate, 7)
    send_row(0, acc)

    pass_on(1, c2p)
    start(vg[:2])
    start(c3p)
    start(c3v)
    arrive(c2v)
    arrive(spreads[1])
    for s, base, planes in ((0, HALF, 2), (1, 0, 6)):
        loop(4, lambda j: products(j, base, planes, lambda p, w, r: vh2[s, p, w, r, :], 0, lambda n, w, r: ph2[s, n, w, r, :], 0))
    wrap((2, 3, 6, 7))

    def local(i, k, r, lpv):
        def at(dk, dr):
            return bb[i, k + dk, pl.ds(r + 8 + dr, 8), :]

        x = at(0, 0)
        s1 = at(-1, 0) + at(1, 0) + at(0, -1) + at(0, 1) + pltpu.roll(x, 1, 1) + pltpu.roll(x, NZ - 1, 1)
        s2 = at(-2, 0) + at(2, 0) + at(0, -2) + at(0, 2) + pltpu.roll(x, 2, 1) + pltpu.roll(x, NZ - 2, 1)
        yb[i, k - 2, pl.ds(r, 8), :] = lpv * x - (2.0 / 3.0) * s1 + (1.0 / 24.0) * s2

    def local_own(i):
        shift = shift_s[i % NB] + 3.75
        for r in range(0, NY, 8):
            for w in (0, 1):
                local(i, 4 + w, r, lp[w, pl.ds(r, 8), :] + shift)

    loop(PAIRS, local_own)

    m1 = take_row(0)
    rr0 = column(m1, KU)
    alpha0 = rr0 / (column(m1, KU + 1) + jnp.sum(wvec * m1 * m1, axis=1, keepdims=True))
    coef = alpha0 * wvec * m1
    for k in range(KU):
        ct[k] = jnp.broadcast_to(column(coef, k), (8, NZ))
    ct[KU] = jnp.broadcast_to(alpha0, (8, NZ))

    def reducer(i):
        scale = [ct[k, pl.ds(i, 1), :] for k in range(KU + 1)]

        def reduced(k, r, fields, ref, place):
            x = bb[i, k, pl.ds(r + 8, 8), :] - scale[KU] * yb[i, k - 2, pl.ds(r, 8), :]
            y = scale[0] * fields[0]
            for c, u in zip(scale[1:KU], fields[1:]):
                y += c * u
            x = x - y
            ref[i, place, pl.ds(r + 8, 8), :] = x
            return x

        return reduced

    def residual_own(i):
        reduced = reducer(i)

        def step(j, sums):
            sums = list(sums)
            for w in (0, 1):
                for t in range(6):
                    r = pl.multiple_of(j * 48 + 8 * t, 8)
                    fields = own_fields(w, pl.ds(r, 8))
                    x = reduced(4 + w, r, fields, rb, w)
                    for k, u in enumerate(fields):
                        sums[k] += u * x
                    sums[KU] += x * x
            return tuple(sums)

        sums = lax.fori_loop(0, 4, step, (zero,) * (KU + 1))
        for k in range(KU + 1):
            put(i, k, sums[k])

        for w in (0, 1):
            rb[i, w, pl.ds(200, 8), :] = rb[i, w, pl.ds(8, 8), :]
        put(i, KU + 1, form_own(i, rb, 0))

    loop(PAIRS, residual_own)

    pass_on(2, c3p)
    arrive(c3v)
    arrive(spreads[2])
    for s, base, planes in ((0, 0, 0), (1, HALF, 8)):
        loop(4, lambda j: products(j, base, planes, lambda p, w, r: vh3[s, p, w, r, :], 0, lambda n, w, r: ph3[s, n, w, r, :], 0))

    def local_beside(i):
        shift = shift_s[i % NB] + 3.75
        for r in range(0, HALF, 8):
            for s, base, planes in ((0, 0, 2), (1, HALF, 6)):
                for w in (0, 1):
                    lpv = ph1[s, r // 24, w, pl.ds(HALF + r % 24, 8), :]
                    local(i, planes + w, base + r, lpv + shift)

    loop(PAIRS, local_beside)

    def residual_beside(i):
        reduced = reducer(i)

        def beside(j):
            for s, base, planes in ((0, 0, 2), (1, HALF, 6)):
                for w in (0, 1):
                    for t in range(6):
                        r0 = pl.multiple_of(j * 48 + 8 * t, 8)
                        at = pl.ds(r0 + base, 8)
                        fields = [pj[a, planes - 2 + w, at, :] for a in range(ATOMS)]
                        fields += [ph1[s, m, w, pl.ds(r0, 8), :] for m in range(NB)]
                        reduced(planes + w, r0 + base, fields, bb, planes + w)

        loop(2, beside)
        put(i, KU + 1, get(i, KU + 1) + form_cross(i, rb, 0))

    loop(PAIRS, residual_beside)
    send_row(1, acc)

    vg[1].wait_recv()
    vg[2].start()
    vg[0].wait_recv()
    vg[2].wait_recv()
    vall[pl.ds(2 * pot, 2)] = v[...]

    def response(i):
        p, n = i // NB, i % NB

        def step(j, sums):
            sums = list(sums)
            for w in (0, 1):
                for t in range(6):
                    r = pl.multiple_of(j * 48 + 8 * t, 8)
                    at = pl.ds(r, 8)
                    orb = psi[n, w, at, :]
                    f0 = orb * bb[i, 4 + w, pl.ds(r + 8, 8), :]
                    f1 = orb * rb[i, w, pl.ds(r + 8, 8), :]
                    for q in range(8):
                        u = vall[q, w, at, :]
                        sums[q] += u * f0
                        sums[8 + q] += u * f1
            return tuple(sums)

        sums = lax.fori_loop(0, 4, step, (zero,) * 16)
        for k in range(16):
            put(i, k, sums[k], racc)

    loop(PAIRS, response)
    send_row(2, racc)

    m2 = take_row(1)
    rr1 = column(m2, KU)
    curve = column(m2, KU + 1) + jnp.sum(wvec * m2 * m2, axis=1, keepdims=True)
    alpha1 = rr1 / (curve - rr1 * (rr1 / rr0) / alpha0)
    first = alpha0 + alpha1 * (rr1 / rr0)
    ct[0] = jnp.broadcast_to(-first, (8, NZ))
    ct[1] = jnp.broadcast_to(-alpha1, (8, NZ))

    def write(i):
        p, n = i // NB, i % NB
        one, two = ct[0, pl.ds(i, 1), :], ct[1, pl.ds(i, 1), :]

        def block(j):
            r = rows(j)
            for w in (0, 1):
                at = pl.ds(r, BLK)
                sol[p, n, w, at, :] = one * bb[i, 4 + w, pl.ds(r + 8, BLK), :] + two * rb[i, w, pl.ds(r + 8, BLK), :]

        loop(8, block)

    loop(PAIRS, write)
    out = pltpu.make_async_copy(sol, sol_h, lsem.at[10])
    out.start()

    m3 = take_row(2)
    each = (-2.0 / CELLS) * (first * m3 + alpha1 * pltpu.roll(m3, NZ - 8, 1))
    for p in range(LOC):
        resp_o[p : p + 1, :] = jnp.sum(each[p * NB : (p + 1) * NB, :8], axis=0, keepdims=True)

    out.wait()
    for c in c1p + c1v + c2p + c2v + c3p + c3v + list(vg):
        c.wait_send()
    for ch in spreads:
        for s in ch:
            s.wait_send()
    for t in range(3):
        rows_copy(t).wait_send()


def shards(band_orbitals, local_potential, band_shift, trial_potentials, projector_blocks, atom_plane, projector_weight):
    anyspec = pl.BlockSpec(memory_space=pltpu.HBM)
    smem = pl.BlockSpec(memory_space=pltpu.SMEM)
    vm = lambda *shape: pltpu.VMEM(shape, F32)
    return pl.pallas_call(
        kernel,
        out_shape=(
            jax.ShapeDtypeStruct((LOC, NB, 2, NY, NZ), F32),
            jax.ShapeDtypeStruct((LOC, 8), F32),
        ),
        in_specs=[anyspec] * 4 + [smem] * 3,
        out_specs=(anyspec, pl.BlockSpec(memory_space=pltpu.VMEM)),
        scratch_shapes=[
            vm(NB, 2, NY, NZ),
            vm(LOC, 2, NY, NZ),
            vm(2, NY, NZ),
            vm(ATOMS, 2, NY, NZ),
            vm(8, 2, NY, NZ),
            vm(2, 2, 2, HALF + 24, NZ),
            vm(2, NB, 2, HALF + 24, NZ),
            vm(2, NB, 2, HALF, NZ),
            vm(2, NB, 2, HALF, NZ),
            vm(2, LOC, 2, HALF, NZ),
            vm(2, LOC, 2, HALF, NZ),
            vm(2, LOC, 2, HALF, NZ),
            vm(PAIRS, 10, NY + 16, NZ),
            vm(PAIRS, 2, NY + 16, NZ),
            vm(PAIRS, 6, NY, NZ),
            vm(ATOMS, 6, NY, NZ),
            vm(LOC, NB, 2, NY, NZ),
            vm(1024, NZ),
            vm(1024, NZ),
            vm(KU + 1, 8, NZ),
            vm(3, 8, NZ),
            vm(3, DOMS, NZ),
            pltpu.SemaphoreType.DMA((11,)),
            pltpu.SemaphoreType.DMA((NSEM,)),
            pltpu.SemaphoreType.DMA((NSEM,)),
            pltpu.SemaphoreType.REGULAR,
        ],
        compiler_params=pltpu.CompilerParams(
            collective_id=0, has_side_effects=True, vmem_limit_bytes=63 * 2**20
        ),
    )(band_orbitals, local_potential, trial_potentials, projector_blocks, band_shift, atom_plane, projector_weight)


def solution(mesh):
    placed = (
        P(None, "dom", None, None),
        P("dom", None, None),
        P(),
        P("pot", "dom", None, None),
        P(),
        P(),
        P(),
    )
    return jax.shard_map(
        shards,
        mesh=mesh,
        in_specs=placed,
        out_specs=(P("pot", None, "dom", None, None), P("pot", None)),
        check_vma=False,
    )
```

```python
import jax
import jax.numpy as jnp
from jax import lax
from jax.experimental import pallas as pl
from jax.experimental.pallas import tpu as pltpu
from jax.sharding import PartitionSpec as P

MESH = pl.DeviceIdType.MESH
F32 = jnp.float32
DOMS, POTS_AXIS = 64, 4
NB, ATOMS, LOC = 4, 8, 2
PAIRS = LOC * NB
NY, NZ, HALF = 192, 128, 96
BLK = 24
KU = ATOMS + NB
CELLS = 128 * 192 * 128
BLOCK_CELLS = 2 * 192 * 128
C1P, C1V, C2P, C2V, C3P, C3V = 0, 2, 4, 6, 8, 10
BCAST = 12
VG = BCAST + 6
ROWS = VG + 3
NSEM = ROWS + 3


def kernel(
    psi_h, lp_h, v_h, proj_h, shift_s, plane_s, weight_s,
    sol_h, resp_o,
    psi, v, lp, proj, vall, stg, ph1, ph2, ph3, vh1, vh2, vh3,
    bb, rb, yb, pj, sol, acc, racc, ct, rowb, slots, lsem, ss, rs, gate,
):
    dom, pot = lax.axis_index("dom"), lax.axis_index("pot")
    right, left = (dom + 1) % DOMS, (dom + DOMS - 1) % DOMS
    mate, part = (pot // 2) * 2 + 1 - pot % 2, (pot + 2) % 4
    plane_xy, zc = dom // 8, dom % 8
    ring = [lax.rem(zc + d, 8) for d in (4, 3, 5, 2, 6, 1, 7, 0)]

    core = pot % 2
    mine = pl.ds(2 * core, 2)
    loads = []
    for s in (0, 1):
        loads.append((psi_h.at[mine, :, pl.ds(s * HALF, HALF)], stg.at[s, :, :, pl.ds(0, HALF)]))
        for b in (0, 1):
            quarter = pl.ds(s * HALF + 24 * (2 * core + b), 24)
            loads.append((lp_h.at[:, quarter], stg.at[s, b, :, pl.ds(HALF, 24)]))
    loads += [
        (v_h, v),
        (psi_h, psi),
        (lp_h, lp),
        (proj_h, proj),
    ]
    loads = [pltpu.make_async_copy(a, b, lsem.at[i]) for i, (a, b) in enumerate(loads)]
    for c in loads:
        c.start()

    bar = pltpu.get_barrier_semaphore()

    def greet(d, p):
        pl.semaphore_signal(bar, inc=1, device_id=(d, p), device_id_type=MESH)

    greet(right, pot)
    greet(left, pot)
    greet(dom, mate)
    greet(dom, part)
    for k in range(1, 8):
        greet(plane_xy * 8 + (zc + k) % 8, pot)
        greet(((plane_xy + k) % 8) * 8 + zc, pot)
    for c in loads[:7]:
        c.wait()
    pl.semaphore_wait(bar, 18)

    def remote(i, src, dst, device):
        return pltpu.make_async_remote_copy(
            src, dst, ss.at[i], rs.at[i], device_id=device, device_id_type=MESH
        )

    low, high = pl.ds(0, HALF), pl.ds(HALF, HALF)
    to = ((right, pot), (left, pot))
    near, far = (low, high), (high, low)
    c1p = [remote(C1P + s, stg.at[s], ph1.at[s, mine], to[s]) for s in (0, 1)]
    c1v = [remote(C1V + s, v.at[:, :, near[s]], vh1.at[s], to[s]) for s in (0, 1)]
    c2p = [remote(C2P + s, psi.at[mine, :, far[s]], ph2.at[s, mine], to[s]) for s in (0, 1)]
    c2v = [remote(C2V + s, v.at[:, :, far[s]], vh2.at[s], to[s]) for s in (0, 1)]
    c3p = [remote(C3P + s, ph1.at[s, mine, :, low], ph3.at[s, mine], to[s]) for s in (0, 1)]
    c3v = [remote(C3V + s, vh1.at[s], vh3.at[s], to[s]) for s in (0, 1)]

    def spread(ch, s):
        own = (ph1, ph2, ph3)[ch].at[s, mine]
        return remote(BCAST + ch * 2 + s, own, own, (dom, mate))

    spreads = [[spread(ch, s) for s in (0, 1)] for ch in range(3)]
    vown, vpart = vall.at[pl.ds(2 * pot, 2)], vall.at[pl.ds(2 * part, 2)]
    vg = (
        remote(VG, v, vown, (dom, mate)),
        remote(VG + 1, v, vown, (dom, part)),
        remote(VG + 2, vpart, vpart, (dom, mate)),
    )

    def start(copies):
        for c in copies:
            c.start()

    def arrive(copies):
        for c in copies:
            c.wait_recv()

    def pass_on(ch, copies):
        arrive(copies)
        start(spreads[ch])

    start(c1p)
    start(c1v)
    for k in range(1, 8):
        pl.semaphore_signal(
            gate, inc=1, device_id=(((plane_xy + k) % 8) * 8 + zc, pot), device_id_type=MESH
        )
    loads[7].wait()
    start(c2p)
    start(c2v)

    acc[...] = jnp.zeros_like(acc)
    lane = lax.broadcasted_iota(jnp.int32, (8, NZ), 1)
    wvec = jnp.where((lane >= ATOMS) & (lane < KU), 1.0 / CELLS, 0.0)
    for a in range(ATOMS):
        wvec = jnp.where(lane == a, weight_s[a] / BLOCK_CELLS, wvec)

    def loop(n, body):
        def step(i, _):
            body(i)
            return 0

        lax.fori_loop(0, n, step, 0)

    def rows(j, base=0):
        return pl.multiple_of(base + j * BLK, 8)

    def products(j, base, planes, vref, vrows, pref, prows):
        at = pl.ds(rows(j, base + 8), BLK)
        for w in (0, 1):
            pots = [vref(p, w, pl.ds(rows(j, vrows), BLK)) for p in range(LOC)]
            for n in range(NB):
                orb = pref(n, w, pl.ds(rows(j, prows), BLK))
                for p in range(LOC):
                    bb[p * NB + n, planes + w, at, :] = pots[p] * orb

    def wrap(planes):
        for i in range(PAIRS):
            for k in planes:
                bb[i, k, pl.ds(200, 8), :] = bb[i, k, pl.ds(8, 8), :]
                bb[i, k, pl.ds(0, 8), :] = bb[i, k, pl.ds(192, 8), :]

    loop(8, lambda j: products(j, 0, 4, lambda p, w, r: v[p, w, r, :], 0, lambda n, w, r: psi[n, w, r, :], 0))
    wrap((4, 5))

    loads[8].wait()
    loads[9].wait()

    def project(a):
        first = plane_s[a]
        pick = []
        for k in range(6):
            x = (2 * dom + k - 2 + 128) % 128
            pick.append([jnp.where(first + w == x, 1.0, 0.0) for w in (0, 1)])

        def block(j):
            for base, ks in ((0, (0, 1, 2, 3)), (HALF, (2, 3, 4, 5))):
                at = pl.ds(rows(j, base), BLK)
                p0, p1 = proj[a, 0, at, :], proj[a, 1, at, :]
                for k in ks:
                    pj[a, k, at, :] = pick[k][0] * p0 + pick[k][1] * p1

        loop(4, block)

    loop(ATOMS, project)

    def put(i, k, value, ref=acc):
        ref[pl.ds(pl.multiple_of(((PAIRS - i) % PAIRS * 16 + k) * 8, 8), 8), :] = value

    def get(i, k):
        return acc[pl.ds(pl.multiple_of(((PAIRS - i) % PAIRS * 16 + k) * 8, 8), 8), :]

    zero = jnp.zeros((8, NZ), F32)

    def own_fields(w, at):
        return [pj[a, 2 + w, at, :] for a in range(ATOMS)] + [psi[m, w, at, :] for m in range(NB)]

    def amounts(i):
        def step(j, sums):
            sums = list(sums)
            for w in (0, 1):
                for t in range(6):
                    r = pl.multiple_of(j * 48 + 8 * t, 8)
                    x = bb[i, 4 + w, pl.ds(r + 8, 8), :]
                    for k, u in enumerate(own_fields(w, pl.ds(r, 8))):
                        sums[k] += u * x
                    sums[KU] += x * x
            return tuple(sums)

        sums = lax.fori_loop(0, 4, step, (zero,) * (KU + 1))
        for k in range(KU + 1):
            put(i, k, sums[k])

    def form_own(i, ref, first):
        shift = shift_s[i % NB] + 3.75
        total = [zero, zero]
        for r in range(0, NY, 8):
            xs = []
            for w in (0, 1):
                x = ref[i, first + w, pl.ds(r + 8, 8), :]
                s1 = ref[i, first + w, pl.ds(r + 9, 8), :] + pltpu.roll(x, NZ - 1, 1)
                s2 = ref[i, first + w, pl.ds(r + 10, 8), :] + pltpu.roll(x, NZ - 2, 1)
                total[w] += x * ((lp[w, pl.ds(r, 8), :] + shift) * x - (4.0 / 3.0) * s1 + (1.0 / 12.0) * s2)
                xs.append(x)
            total[0] -= (4.0 / 3.0) * xs[0] * xs[1]
        return total[0] + total[1]

    def form_cross(i, ref, first):
        total = [zero, zero]
        for r in range(0, HALF, 8):
            x2, x3 = [bb[i, k, pl.ds(r + 8, 8), :] for k in (2, 3)]
            x4, x5 = [ref[i, first + w, pl.ds(r + 8, 8), :] for w in (0, 1)]
            total[0] += x4 * ((1.0 / 12.0) * x2 - (4.0 / 3.0) * x3) + (1.0 / 12.0) * (x3 * x5)
            x4, x5 = [ref[i, first + w, pl.ds(r + 8 + HALF, 8), :] for w in (0, 1)]
            x6, x7 = [bb[i, k, pl.ds(r + 8 + HALF, 8), :] for k in (6, 7)]
            total[1] += x5 * ((1.0 / 12.0) * x7 - (4.0 / 3.0) * x6) + (1.0 / 12.0) * (x4 * x6)
        return total[0] + total[1]

    def send_row(t, ref):
        parts = ref[pl.ds(0, 128, stride=8), :]
        for s in range(1, 8):
            parts += ref[pl.ds(s, 128, stride=8), :]
        row = lax.dot_general(
            jnp.ones((8, NZ), F32), parts, (((1,), (1,)), ((), ())),
            precision=lax.Precision.HIGHEST, preferred_element_type=F32,
        )
        rowb[t] = row
        slots[t, pl.ds(dom, 1), :] = row[0:1]

        def give(xy, places):
            for z in places:
                remote(ROWS + t, rowb.at[t, pl.ds(0, 1)], slots.at[t, pl.ds(dom, 1)], (xy * 8 + z, pot)).start()

        def plane(e, _):
            xj, yj = lax.div(e, 2), lax.rem(e, 2)
            dx = jnp.where(xj == 0, 2, jnp.where(xj == 1, 1, 3 - 3 * (xj - 2)))
            x = lax.rem(lax.div(plane_xy, 2) + dx, 4)
            give(x * 2 + lax.rem(plane_xy + 1 - yj, 2), ring)
            return 0

        lax.fori_loop(0, 7, plane, 0)
        give(plane_xy, ring[:7])

    def rows_copy(t):
        return remote(ROWS + t, slots.at[t, pl.ds(0, DOMS - 1)], slots.at[t, pl.ds(0, DOMS - 1)], (right, pot))

    def take_row(t):
        rows_copy(t).wait_recv()
        total = jnp.sum(slots[t], axis=0, keepdims=True)
        return pltpu.roll(jnp.broadcast_to(total, (8, NZ)), 0, 1, stride=16, stride_axis=0)

    def column(m, k):
        return jnp.sum(jnp.where(lane == k, m, 0.0), axis=1, keepdims=True)

    pass_on(0, c1p)
    loop(PAIRS, amounts)
    loop(PAIRS, lambda i: put(i, KU + 1, form_own(i, bb, 4)))
    arrive(c1v)
    arrive(spreads[0])
    for s, base, planes in ((0, 0, 2), (1, HALF, 6)):
        loop(4, lambda j: products(j, base, planes, lambda p, w, r: vh1[s, p, w, r, :], 0, lambda n, w, r: ph1[s, n, w, r, :], 0))
    loop(PAIRS, lambda i: put(i, KU + 1, get(i, KU + 1) + form_cross(i, bb, 4)))
    pl.semaphore_wait(gate, 7)
    send_row(0, acc)

    pass_on(1, c2p)
    start(vg[:2])
    start(c3p)
    start(c3v)
    arrive(c2v)
    arrive(spreads[1])
    for s, base, planes in ((0, HALF, 2), (1, 0, 6)):
        loop(4, lambda j: products(j, base, planes, lambda p, w, r: vh2[s, p, w, r, :], 0, lambda n, w, r: ph2[s, n, w, r, :], 0))
    wrap((2, 3, 6, 7))

    def local(i, k, r, lpv):
        def at(dk, dr):
            return bb[i, k + dk, pl.ds(r + 8 + dr, 8), :]

        x = at(0, 0)
        s1 = at(-1, 0) + at(1, 0) + at(0, -1) + at(0, 1) + pltpu.roll(x, 1, 1) + pltpu.roll(x, NZ - 1, 1)
        s2 = at(-2, 0) + at(2, 0) + at(0, -2) + at(0, 2) + pltpu.roll(x, 2, 1) + pltpu.roll(x, NZ - 2, 1)
        yb[i, k - 2, pl.ds(r, 8), :] = lpv * x - (2.0 / 3.0) * s1 + (1.0 / 24.0) * s2

    def local_own(i):
        shift = shift_s[i % NB] + 3.75
        for r in range(0, NY, 8):
            for w in (0, 1):
                local(i, 4 + w, r, lp[w, pl.ds(r, 8), :] + shift)

    loop(PAIRS, local_own)

    m1 = take_row(0)
    rr0 = column(m1, KU)
    alpha0 = rr0 / (column(m1, KU + 1) + jnp.sum(wvec * m1 * m1, axis=1, keepdims=True))
    coef = alpha0 * wvec * m1
    for k in range(KU):
        ct[k] = jnp.broadcast_to(column(coef, k), (8, NZ))
    ct[KU] = jnp.broadcast_to(alpha0, (8, NZ))

    def reducer(i):
        scale = [ct[k, pl.ds(i, 1), :] for k in range(KU + 1)]

        def reduced(k, r, fields, ref, place):
            x = bb[i, k, pl.ds(r + 8, 8), :] - scale[KU] * yb[i, k - 2, pl.ds(r, 8), :]
            y = scale[0] * fields[0]
            for c, u in zip(scale[1:KU], fields[1:]):
                y += c * u
            x = x - y
            ref[i, place, pl.ds(r + 8, 8), :] = x
            return x

        return reduced

    def residual_own(i):
        reduced = reducer(i)

        def step(j, sums):
            sums = list(sums)
            for w in (0, 1):
                for t in range(6):
                    r = pl.multiple_of(j * 48 + 8 * t, 8)
                    fields = own_fields(w, pl.ds(r, 8))
                    x = reduced(4 + w, r, fields, rb, w)
                    for k, u in enumerate(fields):
                        sums[k] += u * x
                    sums[KU] += x * x
            return tuple(sums)

        sums = lax.fori_loop(0, 4, step, (zero,) * (KU + 1))
        for k in range(KU + 1):
            put(i, k, sums[k])

        for w in (0, 1):
            rb[i, w, pl.ds(200, 8), :] = rb[i, w, pl.ds(8, 8), :]
        put(i, KU + 1, form_own(i, rb, 0))

    loop(PAIRS, residual_own)

    pass_on(2, c3p)
    arrive(c3v)
    arrive(spreads[2])
    for s, base, planes in ((0, 0, 0), (1, HALF, 8)):
        loop(4, lambda j: products(j, base, planes, lambda p, w, r: vh3[s, p, w, r, :], 0, lambda n, w, r: ph3[s, n, w, r, :], 0))

    def local_beside(i):
        shift = shift_s[i % NB] + 3.75
        for r in range(0, HALF, 8):
            for s, base, planes in ((0, 0, 2), (1, HALF, 6)):
                for w in (0, 1):
                    lpv = ph1[s, r // 24, w, pl.ds(HALF + r % 24, 8), :]
                    local(i, planes + w, base + r, lpv + shift)

    loop(PAIRS, local_beside)

    def residual_beside(i):
        reduced = reducer(i)

        def beside(j):
            for s, base, planes in ((0, 0, 2), (1, HALF, 6)):
                for w in (0, 1):
                    for t in range(6):
                        r0 = pl.multiple_of(j * 48 + 8 * t, 8)
                        at = pl.ds(r0 + base, 8)
                        fields = [pj[a, planes - 2 + w, at, :] for a in range(ATOMS)]
                        fields += [ph1[s, m, w, pl.ds(r0, 8), :] for m in range(NB)]
                        reduced(planes + w, r0 + base, fields, bb, planes + w)

        loop(2, beside)
        put(i, KU + 1, get(i, KU + 1) + form_cross(i, rb, 0))

    loop(PAIRS, residual_beside)
    send_row(1, acc)

    vg[1].wait_recv()
    vg[2].start()
    vg[0].wait_recv()
    vg[2].wait_recv()
    vall[pl.ds(2 * pot, 2)] = v[...]

    def response(i):
        p, n = i // NB, i % NB

        def step(j, sums):
            sums = list(sums)
            for w in (0, 1):
                for t in range(6):
                    r = pl.multiple_of(j * 48 + 8 * t, 8)
                    at = pl.ds(r, 8)
                    orb = psi[n, w, at, :]
                    f0 = orb * bb[i, 4 + w, pl.ds(r + 8, 8), :]
                    f1 = orb * rb[i, w, pl.ds(r + 8, 8), :]
                    for q in range(8):
                        u = vall[q, w, at, :]
                        sums[q] += u * f0
                        sums[8 + q] += u * f1
            return tuple(sums)

        sums = lax.fori_loop(0, 4, step, (zero,) * 16)
        for k in range(16):
            put(i, k, sums[k], racc)

    loop(PAIRS, response)
    send_row(2, racc)

    m2 = take_row(1)
    rr1 = column(m2, KU)
    curve = column(m2, KU + 1) + jnp.sum(wvec * m2 * m2, axis=1, keepdims=True)
    alpha1 = rr1 / (curve - rr1 * (rr1 / rr0) / alpha0)
    first = alpha0 + alpha1 * (rr1 / rr0)
    ct[0] = jnp.broadcast_to(-first, (8, NZ))
    ct[1] = jnp.broadcast_to(-alpha1, (8, NZ))

    def write(i):
        p, n = i // NB, i % NB
        one, two = ct[0, pl.ds(i, 1), :], ct[1, pl.ds(i, 1), :]

        def block(j):
            r = rows(j)
            for w in (0, 1):
                at = pl.ds(r, BLK)
                sol[p, n, w, at, :] = one * bb[i, 4 + w, pl.ds(r + 8, BLK), :] + two * rb[i, w, pl.ds(r + 8, BLK), :]

        loop(8, block)

    loop(PAIRS, write)
    out = pltpu.make_async_copy(sol, sol_h, lsem.at[10])
    out.start()

    m3 = take_row(2)
    each = (-2.0 / CELLS) * (first * m3 + alpha1 * pltpu.roll(m3, NZ - 8, 1))
    for p in range(LOC):
        resp_o[p : p + 1, :] = jnp.sum(each[p * NB : (p + 1) * NB, :8], axis=0, keepdims=True)

    out.wait()
    for c in c1p + c1v + c2p + c2v + c3p + c3v + list(vg):
        c.wait_send()
    for ch in spreads:
        for s in ch:
            s.wait_send()
    for t in range(3):
        rows_copy(t).wait_send()


def shards(band_orbitals, local_potential, band_shift, trial_potentials, projector_blocks, atom_plane, projector_weight):
    anyspec = pl.BlockSpec(memory_space=pltpu.HBM)
    smem = pl.BlockSpec(memory_space=pltpu.SMEM)
    vm = lambda *shape: pltpu.VMEM(shape, F32)
    return pl.pallas_call(
        kernel,
        out_shape=(
            jax.ShapeDtypeStruct((LOC, NB, 2, NY, NZ), F32),
            jax.ShapeDtypeStruct((LOC, 8), F32),
        ),
        in_specs=[anyspec] * 4 + [smem] * 3,
        out_specs=(anyspec, pl.BlockSpec(memory_space=pltpu.VMEM)),
        scratch_shapes=[
            vm(NB, 2, NY, NZ),
            vm(LOC, 2, NY, NZ),
            vm(2, NY, NZ),
            vm(ATOMS, 2, NY, NZ),
            vm(8, 2, NY, NZ),
            vm(2, 2, 2, HALF + 24, NZ),
            vm(2, NB, 2, HALF + 24, NZ),
            vm(2, NB, 2, HALF, NZ),
            vm(2, NB, 2, HALF, NZ),
            vm(2, LOC, 2, HALF, NZ),
            vm(2, LOC, 2, HALF, NZ),
            vm(2, LOC, 2, HALF, NZ),
            vm(PAIRS, 10, NY + 16, NZ),
            vm(PAIRS, 2, NY + 16, NZ),
            vm(PAIRS, 6, NY, NZ),
            vm(ATOMS, 6, NY, NZ),
            vm(LOC, NB, 2, NY, NZ),
            vm(1032, NZ),
            vm(1032, NZ),
            vm(KU + 1, 8, NZ),
            vm(3, 8, NZ),
            vm(3, DOMS, NZ),
            pltpu.SemaphoreType.DMA((11,)),
            pltpu.SemaphoreType.DMA((NSEM,)),
            pltpu.SemaphoreType.DMA((NSEM,)),
            pltpu.SemaphoreType.REGULAR,
        ],
        compiler_params=pltpu.CompilerParams(
            collective_id=0, has_side_effects=True, vmem_limit_bytes=63 * 2**20
        ),
    )(band_orbitals, local_potential, trial_potentials, projector_blocks, band_shift, atom_plane, projector_weight)


def solution(mesh):
    placed = (
        P(None, "dom", None, None),
        P("dom", None, None),
        P(),
        P("pot", "dom", None, None),
        P(),
        P(),
        P(),
    )
    return jax.shard_map(
        shards,
        mesh=mesh,
        in_specs=placed,
        out_specs=(P("pot", None, "dom", None, None), P("pot", None)),
        check_vma=False,
    )
```
